32 devices in a mesh: groups: 2 (over x), tensor: 4 (over y, core), section: 4 (over z).
Axes of the slice: x: 2, y: 2, z: 4, core: 2. Of those that a mesh axis runs over, the one named last changes fastest.
Arguments:
- prompt: bfloat16 [128, 8192], P(('groups', 'section'), 'tensor'), parts along dimension 0, may hold values from -6 to 6
- norm_gain: float32 [8, 8192], P(('groups', 'section')), parts along dimension 0, may hold values from 0.5 to 1.5
- kept_ranks: int32 [8, 3], P(('groups', 'section')), parts along dimension 0, may hold values from 128 to 512, as said below
- gate_left: bfloat16 [8, 512, 8192], P('groups', 'tensor', 'section'), parts along dimension 0, may hold values from -0.0625 to 0.0625
- up_left: bfloat16 [8, 512, 8192], P('groups', 'tensor', 'section'), parts along dimension 0, may hold values from -0.0625 to 0.0625
- gate_right: bfloat16 [8, 512, 14336], P('groups', 'tensor', 'section'), parts along dimension 0, may hold values from -0.375 to 0.375
- up_right: bfloat16 [8, 512, 14336], P('groups', 'tensor', 'section'), parts along dimension 0, may hold values from -0.375 to 0.375
- down_left: bfloat16 [8, 512, 14336], P('groups', 'tensor', 'section'), parts along dimension 0, may hold values from -0.046875 to 0.046875
- down_right: bfloat16 [8, 8192, 512], P('groups', 'tensor', 'section'), parts along dimension 0, may hold values from -0.5 to 0.5
Outputs:
- final_stream: bfloat16 [128, 8192], P(('groups', 'section'), 'tensor'), parts along dimension 0
The draws below stay inside these ranges and needn't reach their ends.
There are 2 independent parts, one for each index of `groups`. The reference program is written for one: setup_inputs(seed, part) draws one part's arguments, and reference() takes and returns one part's arrays. A program takes and returns all parts, laid end to end along the dimension named above; each array names one. Nothing has to cross between parts.
Inputs may be any that keep to these rules, and one draw needn't show every extreme that they name: `kept_ranks`: column 0, 1, 2 holds the rank kept for the gate, up and down matrices; the value 512 occurs in every draw.
All inputs are finite; a program needn't handle non-finite values.
Results may differ from the reference program's by a relative error of at most 0.035.
Values may be sent and summed in bfloat16 or wider, within the bound.
A program may use at most 128 MiB of HBM per device.

```python
import jax
import jax.numpy as jnp
from jax import lax

D = 8192
FF = 14336
RMAX = 512
LAYERS = 4
SPAN = 64


def draw_kept_ranks(key, part):
    key_draw, key_pick = jax.random.split(jax.random.fold_in(key, 7))
    drawn_ranks = jax.random.randint(key_draw, (LAYERS * 3,), RMAX // 4, RMAX + 1)
    chosen = jax.random.randint(key_pick, (), 0, LAYERS * 3)
    flat_ranks = jnp.where(jnp.arange(LAYERS * 3) == chosen, RMAX, drawn_ranks)
    return flat_ranks.reshape(LAYERS, 3).astype(jnp.int32)


def shard_levels(rng, extent, cuts, least, high):
    def one(position, shards_of):
        draws = jax.random.uniform(jax.random.fold_in(jax.random.fold_in(rng, 6), position), (shards_of,), jnp.float32, least / len(cuts), high / len(cuts))
        return jnp.repeat(jnp.exp(draws), extent[position] // shards_of).reshape((-1,) + (1,) * (len(extent) - position - 1))

    gain = one(*cuts[0])
    for cut in cuts[1:]:
        gain = gain * one(*cut)
    return gain


def bell_draw(key, dims, scale, bound, shards=(), kind=jnp.bfloat16):
    entries = jax.random.normal(key, dims, jnp.float32) * scale
    if len(shards) > 0:
        entries = shard_levels(key, dims, shards, -0.22, 0.18) * entries
    return jnp.clip(entries, min=-bound, max=bound).astype(kind)


def setup_inputs(seed: int = 0, part: int = 0) -> dict:
    keys = jax.random.split(jax.random.key(seed), 10)
    own_keys = jax.random.split(jax.random.fold_in(keys[9], part), 10)
    return {
        "prompt": bell_draw(own_keys[0], (SPAN, D), 1.0, 6.0, ((0, 4), (1, 4))),
        "norm_gain": jnp.clip(1.0 + 0.1 * jax.random.normal(own_keys[1], (LAYERS, D), jnp.float32), 0.5, 1.5),
        "kept_ranks": draw_kept_ranks(jax.random.fold_in(jax.random.fold_in(keys[9], part), 71), part),
        "gate_left": bell_draw(own_keys[3], (LAYERS, RMAX, D), D ** -0.5, 0.0625, ((1, 4), (2, 4))),
        "up_left": bell_draw(own_keys[4], (LAYERS, RMAX, D), D ** -0.5, 0.0625, ((1, 4), (2, 4))),
        "gate_right": bell_draw(own_keys[5], (LAYERS, RMAX, FF), (RMAX // 2) ** -0.5, 0.375, ((1, 4), (2, 4))),
        "up_right": bell_draw(own_keys[6], (LAYERS, RMAX, FF), (RMAX // 2) ** -0.5, 0.375, ((1, 4), (2, 4))),
        "down_left": bell_draw(own_keys[7], (LAYERS, RMAX, FF), FF ** -0.5, 0.046875, ((1, 4), (2, 4))),
        "down_right": bell_draw(own_keys[8], (LAYERS, D, RMAX), (RMAX // 4) ** -0.5, 0.5, ((1, 4), (2, 4))),
    }


def reference(prompt, norm_gain, kept_ranks, gate_left, up_left, gate_right, up_right, down_left, down_right):
    stream = prompt
    rank_axis = jnp.arange(RMAX, dtype=jnp.int32)
    for layer_index in range(LAYERS):
        float_stream = stream.astype(jnp.float32)
        variance = lax.optimization_barrier(jnp.mean(float_stream * float_stream, axis=-1, keepdims=True))
        normed = (float_stream * lax.rsqrt(variance + 1e-05) * norm_gain[layer_index]).astype(jnp.bfloat16)
        gate_mask = (rank_axis < kept_ranks[layer_index, 0]).astype(jnp.float32)
        up_mask = (rank_axis < kept_ranks[layer_index, 1]).astype(jnp.float32)
        down_mask = (rank_axis < kept_ranks[layer_index, 2]).astype(jnp.float32)
        gate_low = (jnp.dot(normed, gate_left[layer_index].T, preferred_element_type=jnp.float32) * gate_mask).astype(jnp.bfloat16)
        up_low = (jnp.dot(normed, up_left[layer_index].T, preferred_element_type=jnp.float32) * up_mask).astype(jnp.bfloat16)
        gate_values = jnp.dot(gate_low, gate_right[layer_index], preferred_element_type=jnp.float32)
        up_values = jnp.dot(up_low, up_right[layer_index], preferred_element_type=jnp.float32)
        hidden = (jax.nn.silu(gate_values) * up_values).astype(jnp.bfloat16)
        down_low = (jnp.dot(hidden, down_left[layer_index].T, preferred_element_type=jnp.float32) * down_mask).astype(jnp.bfloat16)
        branch = jnp.dot(down_low, down_right[layer_index].T, preferred_element_type=jnp.float32)
        stream = (float_stream + branch).astype(jnp.bfloat16)
    return stream
```

```python
import functools

import jax
import jax.numpy as jnp
from jax import lax
from jax.experimental import pallas as pl
from jax.experimental.pallas import tpu as pltpu
from jax.sharding import PartitionSpec as P

BF16, F32 = jnp.bfloat16, jnp.float32
AUX, SPREAD, GATE_SUM, GATE_ALL, HID_SUM, HID_ALL, DOWN_SUM, DOWN_ALL, OUT_SUM = range(9)


def contract_last(left_side, right_side):
    return lax.dot_general(
        left_side, right_side, (((1,), (1,)), ((), ())), preferred_element_type=F32
    )


def kernel(
    nt, ns, features,
    prompt, norm_gain, kept, gl_hbm, ul_hbm, gr_hbm, ur_hbm, dl_hbm, dr_hbm,
    out,
    gl, ul, gr, ur, dl, dr,
    gain_out, gain, mask_out, mask,
    own, wide, low_out, low_in, low, val_out, val_in, hid, down_out, down_in,
    dlow_own, dlow, br_out, br_in,
    send, recv, mask_send, mask_recv, load,
):
    t, s = lax.axis_index("tensor"), lax.axis_index("section")
    layers = gl.shape[0]
    fan = nt // ns
    rows, f_block = own.shape
    span = rows * ns
    slab = hid.shape[1]
    rank = gl.shape[1]
    home, part = lax.div(t, fan), lax.rem(t, fan)

    def loads(l):
        return [
            pltpu.make_async_copy(h.at[l], v.at[l], load.at[i, l])
            for i, (h, v) in enumerate(
                ((gl_hbm, gl), (ul_hbm, ul), (gr_hbm, gr), (ur_hbm, ur), (dl_hbm, dl), (dr_hbm, dr))
            )
        ]

    def start_loads(l, carry):
        for copy in loads(l):
            copy.start()
        return carry

    lax.fori_loop(0, layers, start_loads, 0)

    count = nt * ns
    me = t * ns + s
    barrier = pltpu.get_barrier_semaphore()

    def greet(j, carry):
        peer = lax.rem(me + j, count)
        pl.semaphore_signal(
            barrier, inc=1,
            device_id={"tensor": lax.div(peer, ns), "section": lax.rem(peer, ns)},
            device_id_type=pl.DeviceIdType.MESH,
        )
        return carry

    lax.fori_loop(1, count, greet, 0)

    for j in range(ns):
        for kk in range(fan):
            at = (j * fan + kk) * f_block
            gain_out[j, kk] = norm_gain[:, at:at + f_block]
    position = t * rank + lax.broadcasted_iota(jnp.int32, (1, rank), 1)
    for i in range(3):
        mask_out[i] = jnp.where(position < kept[0, i], 1.0, 0.0).astype(F32)
    own[...] = prompt[...]
    pl.semaphore_wait(barrier, count - 1)

    def copy_to(phase, src, dst, dest_slot, src_slot, tt, ss, sems=None):
        sender, receiver = (send, recv) if sems is None else sems
        return pltpu.make_async_remote_copy(
            src_ref=src, dst_ref=dst,
            send_sem=sender.at[phase, dest_slot], recv_sem=receiver.at[phase, src_slot],
            device_id={"tensor": tt, "section": ss}, device_id_type=pl.DeviceIdType.MESH,
        )

    def over_section(phase, src_of, dst_of, sems=None):
        sends, recvs = [], []
        for j in range(1, ns):
            peer = lax.rem(s + j, ns)
            sends.append(copy_to(phase, src_of(peer), dst_of(s), peer, s, t, peer, sems))
            recvs.append(copy_to(phase, src_of(peer), dst_of(peer), peer, peer, t, peer, sems))
        return sends, recvs

    def over_tensor(phase, src_of, dst_of):
        sends, recvs = [], []
        for j in range(1, nt):
            peer = lax.rem(t + j, nt)
            sends.append(copy_to(phase, src_of(peer), dst_of(t), peer, t, peer, s))
            recvs.append(copy_to(phase, src_of(peer), dst_of(peer), peer, peer, peer, s))
        return sends, recvs

    def start(copies):
        for copy in copies:
            copy.start()

    def wait_recv(copies):
        for copy in copies:
            copy.wait_recv()

    def wait_send(copies):
        for copy in copies:
            copy.wait_send()

    def spread(phase, src, dst):
        is_home = home == s

        def each(action):
            for j in range(nt):
                peer = lax.rem(t + j, nt)
                copy = copy_to(phase, src, dst.at[s, part], peer, s * fan + part, peer, home)
                if j == 0:
                    @pl.when(jnp.logical_not(is_home))
                    def _():
                        action(copy)
                else:
                    action(copy)

        def begin():
            each(lambda copy: copy.start())

            @pl.when(is_home)
            def _():
                dst[s, part] = src[...]

        def arrive():
            for j in range(ns):
                for kk in range(fan):
                    copy = copy_to(phase, src, dst.at[j, kk], 0, j * fan + kk, s * fan + kk, j)

                    @pl.when(jnp.logical_not((s * fan + kk == t) & (s == j)))
                    def _():
                        copy.wait_recv()

        def finish():
            each(lambda copy: copy.wait_send())

        return begin, arrive, finish

    gain_send, gain_recv = over_section(AUX, lambda j: gain_out.at[j], lambda j: gain.at[j])
    mask_sends, mask_recvs = over_section(
        0, lambda j: mask_out, lambda j: mask.at[j], (mask_send, mask_recv)
    )
    aux_first = spread(SPREAD, own, wide)
    low_sum = over_section(GATE_SUM, lambda j: low_out.at[j], lambda j: low_in.at[j])
    low_all = over_section(GATE_ALL, lambda j: low.at[s], lambda j: low.at[j])
    hid_sum = over_tensor(HID_SUM, lambda j: val_out.at[j], lambda j: val_in.at[j])
    hid_all = over_tensor(HID_ALL, lambda j: hid.at[t], lambda j: hid.at[j])
    down_sum = over_section(DOWN_SUM, lambda j: down_out.at[j], lambda j: down_in.at[j])
    down_all = spread(DOWN_ALL, dlow_own, dlow)
    out_sum = over_section(OUT_SUM, lambda j: br_out.at[j], lambda j: br_in.at[j])

    start(gain_send)
    start(mask_sends)
    gain[s] = gain_out[s]
    mask[s] = mask_out[...]

    def layer(l, carry):
        begin, arrive, finish = aux_first
        begin()

        @pl.when(l == 0)
        def _():
            wait_recv(gain_recv)
            wait_recv(mask_recvs)

        weights = loads(l)
        weights[0].wait()
        weights[1].wait()
        arrive()

        gate_part = jnp.zeros((span, rank), F32)
        up_part = jnp.zeros((span, rank), F32)
        squares = jnp.zeros((span, 1), F32)
        for kk in range(fan):
            piece = wide[:, kk].reshape(span, f_block).astype(F32)
            squares += jnp.sum(piece * piece, axis=-1, keepdims=True)
            scaled = (piece * gain[l, kk]).astype(BF16)
            at = kk * f_block
            gate_part += contract_last(scaled, gl[l, :, at:at + f_block])
            up_part += contract_last(scaled, ul[l, :, at:at + f_block])
        low_out[:, 0] = gate_part.reshape(ns, rows, rank)
        low_out[:, 1] = up_part.reshape(ns, rows, rank)
        low_out[:, 2] = jnp.broadcast_to(squares, (span, rank)).reshape(ns, rows, rank)
        start(low_sum[0])
        low_in[s] = low_out[s]
        wait_recv(low_sum[1])
        total = jnp.sum(low_in[...], axis=0)
        scale = lax.rsqrt(total[2] / features + 1e-05)
        low[s, 0] = (total[0] * scale * mask[l, 0]).astype(BF16)
        low[s, 1] = (total[1] * scale * mask[l, 1]).astype(BF16)
        start(low_all[0])
        weights[2].wait()
        weights[3].wait()
        wait_recv(low_all[1])

        width = gr.shape[2]
        gate_low = low[:, 0].reshape(span, rank)
        up_low = low[:, 1].reshape(span, rank)
        gate_values = jnp.dot(gate_low, gr[l], preferred_element_type=F32)
        val_out[:, 0] = gate_values.astype(BF16).reshape(nt, slab, width)
        up_values = jnp.dot(up_low, ur[l], preferred_element_type=F32)
        val_out[:, 1] = up_values.astype(BF16).reshape(nt, slab, width)
        start(hid_sum[0])
        val_in[t] = val_out[t]
        wait_recv(hid_sum[1])
        gate_sum = jnp.sum(val_in[:, 0].astype(F32), axis=0)
        up_sum = jnp.sum(val_in[:, 1].astype(F32), axis=0)
        hid[t] = (gate_sum / (1.0 + jnp.exp(-gate_sum)) * up_sum).astype(BF16)
        start(hid_all[0])
        weights[4].wait()
        wait_recv(hid_all[1])

        down_out[...] = contract_last(hid[...].reshape(span, width), dl[l]).reshape(ns, rows, rank)
        start(down_sum[0])
        down_in[s] = down_out[s]
        wait_recv(down_sum[1])
        dlow_own[...] = (jnp.sum(down_in[...], axis=0) * mask[l, 2]).astype(BF16)
        begin_down, arrive_down, finish_down = down_all
        begin_down()
        weights[5].wait()
        arrive_down()

        branch = jnp.zeros((span, f_block), F32)
        for kk in range(fan):
            at = kk * rank
            branch += contract_last(dlow[:, kk].reshape(span, rank), dr[l, :, at:at + rank])
        br_out[...] = branch.astype(BF16).reshape(ns, rows, f_block)
        start(out_sum[0])
        br_in[s] = br_out[s]
        wait_recv(out_sum[1])
        finish()
        own[...] = (own[...].astype(F32) + jnp.sum(br_in[...].astype(F32), axis=0)).astype(BF16)

        wait_send(low_sum[0])
        wait_send(low_all[0])
        wait_send(hid_sum[0])
        wait_send(hid_all[0])
        wait_send(down_sum[0])
        finish_down()
        wait_send(out_sum[0])
        return carry

    lax.fori_loop(0, layers, layer, 0)
    wait_send(gain_send)
    wait_send(mask_sends)
    out[...] = own[...]


def body(
    nt, ns,
    prompt, norm_gain, kept_ranks, gate_left, up_left, gate_right, up_right, down_left, down_right,
):
    rows, f_block = prompt.shape
    layers, rank, _ = gate_left.shape
    width = gate_right.shape[2]
    fan = nt // ns
    span = rows * ns
    slab = span // nt
    slots = max(nt, ns, ns * fan)
    weights = (gate_left, up_left, gate_right, up_right, down_left, down_right)
    vmem, hbm = pl.BlockSpec(memory_space=pltpu.VMEM), pl.BlockSpec(memory_space=pl.ANY)
    return pl.pallas_call(
        functools.partial(kernel, nt, ns, float(norm_gain.shape[1])),
        out_shape=jax.ShapeDtypeStruct((rows, f_block), BF16),
        in_specs=[vmem, vmem, pl.BlockSpec(memory_space=pltpu.SMEM)] + [hbm] * 6,
        out_specs=vmem,
        scratch_shapes=[pltpu.VMEM(w.shape, BF16) for w in weights] + [
            pltpu.VMEM((ns, fan, 1, f_block), F32),
            pltpu.VMEM((ns, fan, 1, f_block), F32),
            pltpu.VMEM((3, 1, rank), F32),
            pltpu.VMEM((ns, 3, 1, rank), F32),
            pltpu.VMEM((rows, f_block), BF16),
            pltpu.VMEM((ns, fan, rows, f_block), BF16),
            pltpu.VMEM((ns, 3, rows, rank), F32),
            pltpu.VMEM((ns, 3, rows, rank), F32),
            pltpu.VMEM((ns, 2, rows, rank), BF16),
            pltpu.VMEM((nt, 2, slab, width), BF16),
            pltpu.VMEM((nt, 2, slab, width), BF16),
            pltpu.VMEM((nt, slab, width), BF16),
            pltpu.VMEM((ns, rows, rank), F32),
            pltpu.VMEM((ns, rows, rank), F32),
            pltpu.VMEM((rows, rank), BF16),
            pltpu.VMEM((ns, fan, rows, rank), BF16),
            pltpu.VMEM((ns, rows, f_block), BF16),
            pltpu.VMEM((ns, rows, f_block), BF16),
            pltpu.SemaphoreType.DMA((9, slots)),
            pltpu.SemaphoreType.DMA((9, slots)),
            pltpu.SemaphoreType.DMA((1, slots)),
            pltpu.SemaphoreType.DMA((1, slots)),
            pltpu.SemaphoreType.DMA((6, layers)),
        ],
        compiler_params=pltpu.CompilerParams(
            collective_id=0, has_side_effects=True, vmem_limit_bytes=52 * 1024 * 1024
        ),
        cost_estimate=pl.CostEstimate(
            flops=2 * span * sum(w.size for w in weights),
            bytes_accessed=2 * sum(w.size for w in weights),
            transcendentals=span * width * layers // nt,
        ),
    )(prompt, norm_gain, kept_ranks, *weights)


def solution(mesh):
    in_specs = (
        P(("groups", "section"), "tensor"),
        P(("groups", "section"), None),
        P(("groups", "section"), None),
    ) + (P("groups", "tensor", "section"),) * 6
    return jax.shard_map(
        functools.partial(body, mesh.shape["tensor"], mesh.shape["section"]),
        mesh=mesh, in_specs=in_specs, out_specs=P(("groups", "section"), "tensor"), check_vma=False,
    )
```

```python
import functools

import jax
import jax.numpy as jnp
from jax import lax
from jax.experimental import pallas as pl
from jax.experimental.pallas import tpu as pltpu
from jax.sharding import PartitionSpec as P

BF16, F32 = jnp.bfloat16, jnp.float32
AUX, SPREAD, GATHER, GATE_SUM, GATE_ALL, PAIR, GATE_VALUES, UP_VALUES = range(8)
HID_ALL, DOWN_SUM, DOWN_ALL, OUT_SUM, PHASES = range(8, 13)


def contract_last(left_side, right_side):
    return lax.dot_general(
        left_side, right_side, (((1,), (1,)), ((), ())), preferred_element_type=F32
    )


def kernel(
    nt, ns, features,
    prompt, norm_gain, kept, gl_hbm, ul_hbm, gr_hbm, ur_hbm, dl_hbm, dr_hbm,
    out,
    gl, ul, gr, ur, dl, dr,
    gain_out, gain, mask_out, mask,
    own, wide, low_out, low_in, low, val_out, pair_in, val_mid, val_in, hid, down_out, down_in,
    dlow_own, dlow, br_out, br_in,
    send, recv, mask_send, mask_recv, load,
):
    t, s = lax.axis_index("tensor"), lax.axis_index("section")
    layers = gl.shape[0]
    fan = nt // ns
    _, rows, piece = own.shape
    f_block = piece * nt
    span = rows * ns
    slab = hid.shape[1]
    rank = gl.shape[1]
    home, part = lax.div(t, fan), lax.rem(t, fan)
    chips = nt // 2
    chip, core = lax.div(t, 2), lax.rem(t, 2)
    sibling = chip * 2 + 1 - core

    def loads(l):
        return [
            pltpu.make_async_copy(h.at[l], v.at[l], load.at[i, l])
            for i, (h, v) in enumerate(
                ((gl_hbm, gl), (ul_hbm, ul), (gr_hbm, gr), (ur_hbm, ur), (dl_hbm, dl), (dr_hbm, dr))
            )
        ]

    def start_loads(l, carry):
        for copy in loads(l):
            copy.start()
        return carry

    lax.fori_loop(0, layers, start_loads, 0)

    count = nt * ns
    me = t * ns + s
    barrier = pltpu.get_barrier_semaphore()

    def greet(j, carry):
        peer = lax.rem(me + j, count)
        pl.semaphore_signal(
            barrier, inc=1,
            device_id={"tensor": lax.div(peer, ns), "section": lax.rem(peer, ns)},
            device_id_type=pl.DeviceIdType.MESH,
        )
        return carry

    lax.fori_loop(1, count, greet, 0)

    for j in range(ns):
        for kk in range(fan):
            at = (j * fan + kk) * f_block
            gain_out[j, kk] = norm_gain[:, at:at + f_block]
    position = t * rank + lax.broadcasted_iota(jnp.int32, (1, rank), 1)
    for i in range(3):
        mask_out[i] = jnp.where(position < kept[0, i], 1.0, 0.0).astype(F32)
    for p in range(nt):
        own[p] = prompt[:, p * piece:(p + 1) * piece]
    pl.semaphore_wait(barrier, count - 1)

    def copy_to(phase, src, dst, dest_slot, src_slot, tt, ss, sems=None):
        sender, receiver = (send, recv) if sems is None else sems
        return pltpu.make_async_remote_copy(
            src_ref=src, dst_ref=dst,
            send_sem=sender.at[phase, dest_slot], recv_sem=receiver.at[phase, src_slot],
            device_id={"tensor": tt, "section": ss}, device_id_type=pl.DeviceIdType.MESH,
        )

    def over_section(phase, src_of, dst_of, sems=None):
        sends, recvs = [], []
        for j in range(1, ns):
            peer = lax.rem(s + j, ns)
            sends.append(copy_to(phase, src_of(peer), dst_of(s), peer, s, t, peer, sems))
            recvs.append(copy_to(phase, src_of(peer), dst_of(peer), peer, peer, t, peer, sems))
        return sends, recvs

    def over_tensor(phase, src_of, dst_of):
        sends, recvs = [], []
        for j in range(1, nt):
            peer = lax.rem(t + j, nt)
            sends.append(copy_to(phase, src_of(peer), dst_of(t), peer, t, peer, s))
            recvs.append(copy_to(phase, src_of(peer), dst_of(peer), peer, peer, peer, s))
        return sends, recvs

    def pair_copies(i):
        return copy_to(PAIR, val_out.at[i, 1 - core], pair_in.at[i], i, i, sibling, s)

    def over_chips(phase, i):
        sends, recvs = [], []
        for j in range(1, chips):
            peer = lax.rem(chip + j, chips)
            src, to = val_mid.at[i, peer], peer * 2 + core
            sends.append(copy_to(phase, src, val_in.at[i, chip], peer, chip, to, s))
            recvs.append(copy_to(phase, src, val_in.at[i, peer], peer, peer, to, s))
        return sends, recvs

    def start(copies):
        for copy in copies:
            copy.start()

    def wait_recv(copies):
        for copy in copies:
            copy.wait_recv()

    def wait_send(copies):
        for copy in copies:
            copy.wait_send()

    def spread(phase, src_of, dst_of):
        is_home = home == s

        def each(action):
            for j in range(nt):
                peer = lax.rem(t + j, nt)
                copy = copy_to(
                    phase, src_of(peer), dst_of(peer).at[s, part], peer, s * fan + part, peer, home
                )
                if j == 0:
                    @pl.when(jnp.logical_not(is_home))
                    def _():
                        action(copy)
                else:
                    action(copy)

        def begin():
            each(lambda copy: copy.start())

            @pl.when(is_home)
            def _():
                dst_of(t)[s, part] = src_of(t)[...]

        def arrive():
            for j in range(ns):
                for kk in range(fan):
                    copy = copy_to(
                        phase, src_of(t), dst_of(t).at[j, kk], 0, j * fan + kk, s * fan + kk, j
                    )

                    @pl.when(jnp.logical_not((s * fan + kk == t) & (s == j)))
                    def _():
                        copy.wait_recv()

        def finish():
            each(lambda copy: copy.wait_send())

        return begin, arrive, finish

    gain_send, gain_recv = over_section(AUX, lambda j: gain_out.at[j], lambda j: gain.at[j])
    mask_sends, mask_recvs = over_section(
        0, lambda j: mask_out, lambda j: mask.at[j], (mask_send, mask_recv)
    )
    aux_first = spread(SPREAD, lambda j: own.at[j], lambda j: wide.at[j])
    gather = over_tensor(GATHER, lambda j: wide.at[t], lambda j: wide.at[j])
    low_sum = over_section(GATE_SUM, lambda j: low_out.at[j], lambda j: low_in.at[j])
    low_all = over_section(GATE_ALL, lambda j: low.at[s], lambda j: low.at[j])
    pairs = [pair_copies(i) for i in range(2)]
    values = [over_chips(GATE_VALUES, 0), over_chips(UP_VALUES, 1)]
    hid_all = over_tensor(HID_ALL, lambda j: hid.at[t], lambda j: hid.at[j])
    down_sum = over_section(DOWN_SUM, lambda j: down_out.at[j], lambda j: down_in.at[j])
    down_all = spread(DOWN_ALL, lambda j: dlow_own, lambda j: dlow)
    out_sum = over_section(OUT_SUM, lambda j: br_out.at[j], lambda j: br_in.at[j])

    start(gain_send)
    start(mask_sends)
    gain[s] = gain_out[s]
    mask[s] = mask_out[...]

    def layer(l, carry):
        begin, arrive, finish = aux_first
        begin()

        @pl.when(l == 0)
        def _():
            wait_recv(gain_recv)
            wait_recv(mask_recvs)

        weights = loads(l)
        weights[0].wait()
        weights[1].wait()
        arrive()

        start(gather[0])
        gate_part = jnp.zeros((span, rank), F32)
        up_part = jnp.zeros((span, rank), F32)
        squares = jnp.zeros((span, 1), F32)
        wait_recv(gather[1])
        for p in range(nt):
            for kk in range(fan):
                values_here = wide[p, :, kk].reshape(span, piece).astype(F32)
                squares += jnp.sum(values_here * values_here, axis=-1, keepdims=True)
                at = kk * f_block + p * piece
                gains = gain[l, kk, :, p * piece:(p + 1) * piece]
                scaled = (values_here * gains).astype(BF16)
                gate_part += contract_last(scaled, gl[l, :, at:at + piece])
                up_part += contract_last(scaled, ul[l, :, at:at + piece])
        low_out[:, 0] = gate_part.astype(BF16).reshape(ns, rows, rank)
        low_out[:, 1] = up_part.astype(BF16).reshape(ns, rows, rank)
        low_out[:, 2] = jnp.broadcast_to(squares, (span, rank)).astype(BF16).reshape(ns, rows, rank)
        start(low_sum[0])
        low_in[s] = low_out[s]
        wait_recv(low_sum[1])
        total = jnp.sum(low_in[...].astype(F32), axis=0)
        scale = lax.rsqrt(total[2] / features + 1e-05)
        low[s, 0] = (total[0] * scale * mask[l, 0]).astype(BF16)
        low[s, 1] = (total[1] * scale * mask[l, 1]).astype(BF16)
        start(low_all[0])
        weights[2].wait()
        weights[3].wait()
        wait_recv(low_all[1])

        width = gr.shape[2]
        gate_low = low[:, 0].reshape(span, rank)
        up_low = low[:, 1].reshape(span, rank)
        wait_send(gather[0])
        for i, (narrow, right) in enumerate(((gate_low, gr), (up_low, ur))):
            product = jnp.dot(narrow, right[l], preferred_element_type=F32).astype(BF16)
            for j in range(nt):
                val_out[i, j % 2, j // 2] = product[j * slab:(j + 1) * slab]
            pairs[i].start()
        sums = []
        for i in range(2):
            pairs[i].wait_recv()
            for j in range(chips):
                val_mid[i, j] = (
                    val_out[i, core, j].astype(F32) + pair_in[i, j].astype(F32)
                ).astype(BF16)
            start(values[i][0])
            val_in[i, chip] = val_mid[i, chip]
        for i in range(2):
            wait_recv(values[i][1])
            sums.append(jnp.sum(val_in[i].astype(F32), axis=0))
        gate_sum, up_sum = sums
        hid[t] = (gate_sum / (1.0 + jnp.exp(-gate_sum)) * up_sum).astype(BF16)
        start(hid_all[0])
        weights[4].wait()
        wait_recv(hid_all[1])

        down_out[...] = contract_last(
            hid[...].reshape(span, width), dl[l]
        ).astype(BF16).reshape(ns, rows, rank)
        start(down_sum[0])
        down_in[s] = down_out[s]
        wait_recv(down_sum[1])
        dlow_own[...] = (jnp.sum(down_in[...].astype(F32), axis=0) * mask[l, 2]).astype(BF16)
        begin_down, arrive_down, finish_down = down_all
        begin_down()
        weights[5].wait()
        arrive_down()

        branch = jnp.zeros((span, f_block), F32)
        for kk in range(fan):
            at = kk * rank
            branch += contract_last(dlow[:, kk].reshape(span, rank), dr[l, :, at:at + rank])
        br_out[...] = branch.astype(BF16).reshape(ns, rows, f_block)
        start(out_sum[0])
        br_in[s] = br_out[s]
        wait_recv(out_sum[1])
        finish()
        for p in range(nt):
            added = jnp.sum(br_in[:, :, p * piece:(p + 1) * piece].astype(F32), axis=0)
            own[p] = (own[p].astype(F32) + added).astype(BF16)

        wait_send(low_sum[0])
        wait_send(low_all[0])
        for i in range(2):
            pairs[i].wait_send()
            wait_send(values[i][0])
        wait_send(hid_all[0])
        wait_send(down_sum[0])
        finish_down()
        wait_send(out_sum[0])
        return carry

    lax.fori_loop(0, layers, layer, 0)
    wait_send(gain_send)
    wait_send(mask_sends)
    for p in range(nt):
        out[:, p * piece:(p + 1) * piece] = own[p]


def body(
    nt, ns,
    prompt, norm_gain, kept_ranks, gate_left, up_left, gate_right, up_right, down_left, down_right,
):
    rows, f_block = prompt.shape
    layers, rank, _ = gate_left.shape
    width = gate_right.shape[2]
    fan = nt // ns
    span = rows * ns
    slab = span // nt
    piece, chips = f_block // nt, nt // 2
    slots = max(nt, ns, ns * fan)
    weights = (gate_left, up_left, gate_right, up_right, down_left, down_right)
    vmem, hbm = pl.BlockSpec(memory_space=pltpu.VMEM), pl.BlockSpec(memory_space=pl.ANY)
    return pl.pallas_call(
        functools.partial(kernel, nt, ns, float(norm_gain.shape[1])),
        out_shape=jax.ShapeDtypeStruct((rows, f_block), BF16),
        in_specs=[vmem, vmem, pl.BlockSpec(memory_space=pltpu.SMEM)] + [hbm] * 6,
        out_specs=vmem,
        scratch_shapes=[pltpu.VMEM(w.shape, BF16) for w in weights] + [
            pltpu.VMEM((ns, fan, 1, f_block), F32),
            pltpu.VMEM((ns, fan, 1, f_block), F32),
            pltpu.VMEM((3, 1, rank), F32),
            pltpu.VMEM((ns, 3, 1, rank), F32),
            pltpu.VMEM((nt, rows, piece), BF16),
            pltpu.VMEM((nt, ns, fan, rows, piece), BF16),
            pltpu.VMEM((ns, 3, rows, rank), BF16),
            pltpu.VMEM((ns, 3, rows, rank), BF16),
            pltpu.VMEM((ns, 2, rows, rank), BF16),
            pltpu.VMEM((2, 2, chips, slab, width), BF16),
            pltpu.VMEM((2, chips, slab, width), BF16),
            pltpu.VMEM((2, chips, slab, width), BF16),
            pltpu.VMEM((2, chips, slab, width), BF16),
            pltpu.VMEM((nt, slab, width), BF16),
            pltpu.VMEM((ns, rows, rank), BF16),
            pltpu.VMEM((ns, rows, rank), BF16),
            pltpu.VMEM((rows, rank), BF16),
            pltpu.VMEM((ns, fan, rows, rank), BF16),
            pltpu.VMEM((ns, rows, f_block), BF16),
            pltpu.VMEM((ns, rows, f_block), BF16),
            pltpu.SemaphoreType.DMA((PHASES, slots)),
            pltpu.SemaphoreType.DMA((PHASES, slots)),
            pltpu.SemaphoreType.DMA((1, slots)),
            pltpu.SemaphoreType.DMA((1, slots)),
            pltpu.SemaphoreType.DMA((6, layers)),
        ],
        compiler_params=pltpu.CompilerParams(
            collective_id=0, has_side_effects=True, vmem_limit_bytes=52 * 1024 * 1024
        ),
        cost_estimate=pl.CostEstimate(
            flops=2 * span * sum(w.size for w in weights),
            bytes_accessed=2 * sum(w.size for w in weights),
            transcendentals=span * width * layers // nt,
        ),
    )(prompt, norm_gain, kept_ranks, *weights)


def solution(mesh):
    in_specs = (
        P(("groups", "section"), "tensor"),
        P(("groups", "section"), None),
        P(("groups", "section"), None),
    ) + (P("groups", "tensor", "section"),) * 6
    return jax.shard_map(
        functools.partial(body, mesh.shape["tensor"], mesh.shape["section"]),
        mesh=mesh, in_specs=in_specs, out_specs=P(("groups", "section"), "tensor"), check_vma=False,
    )
```

```python
import functools

import jax
import jax.numpy as jnp
from jax import lax
from jax.experimental import pallas as pl
from jax.experimental.pallas import tpu as pltpu
from jax.sharding import PartitionSpec as P

BF16, F32 = jnp.bfloat16, jnp.float32
AUX, SPREAD, GATHER, GATE_SUM, SQUARES, PAIR, GATE_VALUES, UP_VALUES = range(8)
HID_ALL, DOWN, OUT_SUM, PHASES = range(8, 12)


def contract_last(left_side, right_side):
    return lax.dot_general(
        left_side, right_side, (((1,), (1,)), ((), ())), preferred_element_type=F32
    )


def kernel(
    nt, ns, features,
    prompt, norm_gain, kept, gl_hbm, ul_hbm, gr_hbm, ur_hbm, dl_hbm, dr_hbm,
    out,
    gl, ul, gr, ur, dl, dr,
    gain_out, gain, mask_out, mask,
    own, wide, low_out, low_in, sq_out, sq_in, val_out, pair_in, val_mid, val_in, hid,
    dlow_own, dlow, br_out, br_in,
    send, recv, mask_send, mask_recv, load,
):
    t, s = lax.axis_index("tensor"), lax.axis_index("section")
    layers = gl.shape[0]
    fan = nt // ns
    _, rows, piece = own.shape
    f_block = piece * nt
    span = rows * ns
    slab = hid.shape[1]
    rank = gl.shape[1]
    home, part = lax.div(t, fan), lax.rem(t, fan)
    chips = nt // 2
    chip, core = lax.div(t, 2), lax.rem(t, 2)
    sibling = chip * 2 + 1 - core

    def loads(l):
        return [
            pltpu.make_async_copy(h.at[l], v.at[l], load.at[i, l])
            for i, (h, v) in enumerate(
                ((gl_hbm, gl), (ul_hbm, ul), (gr_hbm, gr), (ur_hbm, ur), (dl_hbm, dl), (dr_hbm, dr))
            )
        ]

    def start_loads(l, carry):
        for copy in loads(l):
            copy.start()
        return carry

    lax.fori_loop(0, layers, start_loads, 0)

    count = nt * ns
    me = t * ns + s
    barrier = pltpu.get_barrier_semaphore()

    def greet(j, carry):
        peer = lax.rem(me + j, count)
        pl.semaphore_signal(
            barrier, inc=1,
            device_id={"tensor": lax.div(peer, ns), "section": lax.rem(peer, ns)},
            device_id_type=pl.DeviceIdType.MESH,
        )
        return carry

    lax.fori_loop(1, count, greet, 0)

    for j in range(ns):
        for kk in range(fan):
            at = (j * fan + kk) * f_block
            gain_out[j, kk] = norm_gain[:, at:at + f_block]
    position = t * rank + lax.broadcasted_iota(jnp.int32, (1, rank), 1)
    for i in range(3):
        mask_out[i] = jnp.where(position < kept[0, i], 1.0, 0.0).astype(F32)
    for p in range(nt):
        own[p] = prompt[:, p * piece:(p + 1) * piece]
    pl.semaphore_wait(barrier, count - 1)

    def copy_to(phase, src, dst, dest_slot, src_slot, tt, ss, sems=None):
        sender, receiver = (send, recv) if sems is None else sems
        return pltpu.make_async_remote_copy(
            src_ref=src, dst_ref=dst,
            send_sem=sender.at[phase, dest_slot], recv_sem=receiver.at[phase, src_slot],
            device_id={"tensor": tt, "section": ss}, device_id_type=pl.DeviceIdType.MESH,
        )

    def over_section(phase, src_of, dst_of, sems=None):
        sends, recvs = [], []
        for j in range(1, ns):
            peer = lax.rem(s + j, ns)
            sends.append(copy_to(phase, src_of(peer), dst_of(s), peer, s, t, peer, sems))
            recvs.append(copy_to(phase, src_of(peer), dst_of(peer), peer, peer, t, peer, sems))
        return sends, recvs

    def over_tensor(phase, src_of, dst_of):
        sends, recvs = [], []
        for j in range(1, nt):
            peer = lax.rem(t + j, nt)
            sends.append(copy_to(phase, src_of(peer), dst_of(t), peer, t, peer, s))
            recvs.append(copy_to(phase, src_of(peer), dst_of(peer), peer, peer, peer, s))
        return sends, recvs

    def pair_copies(i):
        return copy_to(PAIR, val_out.at[i, 1 - core], pair_in.at[i], i, i, sibling, s)

    def over_chips(phase, i):
        sends, recvs = [], []
        for j in range(1, chips):
            peer = lax.rem(chip + j, chips)
            src, to = val_mid.at[i, peer], peer * 2 + core
            sends.append(copy_to(phase, src, val_in.at[i, chip], peer, chip, to, s))
            recvs.append(copy_to(phase, src, val_in.at[i, peer], peer, peer, to, s))
        return sends, recvs

    def start(copies):
        for copy in copies:
            copy.start()

    def wait_recv(copies):
        for copy in copies:
            copy.wait_recv()

    def wait_send(copies):
        for copy in copies:
            copy.wait_send()

    def spread(phase, src_of, dst_of):
        is_home = home == s

        def each(action):
            for j in range(nt):
                peer = lax.rem(t + j, nt)
                copy = copy_to(
                    phase, src_of(peer), dst_of(peer).at[s, part], peer, s * fan + part, peer, home
                )
                if j == 0:
                    @pl.when(jnp.logical_not(is_home))
                    def _():
                        action(copy)
                else:
                    action(copy)

        def begin():
            each(lambda copy: copy.start())

            @pl.when(is_home)
            def _():
                dst_of(t)[s, part] = src_of(t)[...]

        def arrive():
            for j in range(ns):
                for kk in range(fan):
                    copy = copy_to(
                        phase, src_of(t), dst_of(t).at[j, kk], 0, j * fan + kk, s * fan + kk, j
                    )

                    @pl.when(jnp.logical_not((s * fan + kk == t) & (s == j)))
                    def _():
                        copy.wait_recv()

        def finish():
            each(lambda copy: copy.wait_send())

        return begin, arrive, finish

    gain_send, gain_recv = over_section(AUX, lambda j: gain_out.at[j], lambda j: gain.at[j])
    mask_sends, mask_recvs = over_section(
        0, lambda j: mask_out, lambda j: mask.at[j], (mask_send, mask_recv)
    )
    aux_first = spread(SPREAD, lambda j: own.at[j], lambda j: wide.at[j])
    gather = over_tensor(GATHER, lambda j: wide.at[t], lambda j: wide.at[j])
    low_sum = over_section(GATE_SUM, lambda j: low_out, lambda j: low_in.at[j])
    sq_sum = over_section(SQUARES, lambda j: sq_out, lambda j: sq_in.at[j])
    pairs = [pair_copies(i) for i in range(2)]
    values = [over_chips(GATE_VALUES, 0), over_chips(UP_VALUES, 1)]
    hid_all = over_tensor(HID_ALL, lambda j: hid.at[t], lambda j: hid.at[j])
    down_all = spread(DOWN, lambda j: dlow_own, lambda j: dlow)
    out_sum = over_section(OUT_SUM, lambda j: br_out.at[j], lambda j: br_in.at[j])

    start(gain_send)
    start(mask_sends)
    gain[s] = gain_out[s]
    mask[s] = mask_out[...]

    def layer(l, carry):
        begin, arrive, finish = aux_first
        begin()

        @pl.when(l == 0)
        def _():
            wait_recv(gain_recv)
            wait_recv(mask_recvs)

        weights = loads(l)
        weights[0].wait()
        weights[1].wait()
        arrive()

        start(gather[0])
        gate_part = jnp.zeros((span, rank), F32)
        up_part = jnp.zeros((span, rank), F32)
        squares = jnp.zeros((span, 1), F32)
        wait_recv(gather[1])
        for p in range(nt):
            for kk in range(fan):
                values_here = wide[p, :, kk].reshape(span, piece).astype(F32)
                squares += jnp.sum(values_here * values_here, axis=-1, keepdims=True)
                at = kk * f_block + p * piece
                gains = gain[l, kk, :, p * piece:(p + 1) * piece]
                scaled = (values_here * gains).astype(BF16)
                gate_part += contract_last(scaled, gl[l, :, at:at + piece])
                up_part += contract_last(scaled, ul[l, :, at:at + piece])
        low_out[0] = gate_part.astype(BF16)
        low_out[1] = up_part.astype(BF16)
        diagonal = lax.broadcasted_iota(jnp.int32, (span, span), 0) == lax.broadcasted_iota(
            jnp.int32, (span, span), 1
        )
        sq_out[...] = jnp.sum(jnp.where(diagonal, squares, 0.0), axis=0, keepdims=True)
        start(sq_sum[0])
        start(low_sum[0])
        low_in[s] = low_out[...]
        sq_in[s] = sq_out[...]
        wait_recv(sq_sum[1])
        square_row = jnp.sum(sq_in[...], axis=0)
        square = jnp.sum(jnp.where(diagonal, square_row, 0.0), axis=1, keepdims=True)
        scale = lax.rsqrt(square / features + 1e-05)
        weights[2].wait()
        weights[3].wait()
        wait_recv(low_sum[1])
        total = jnp.sum(low_in[...].astype(F32), axis=0)
        gate_low = (total[0] * scale * mask[l, 0]).astype(BF16)
        up_low = (total[1] * scale * mask[l, 1]).astype(BF16)

        width = gr.shape[2]
        wait_send(gather[0])
        for i, (narrow, right) in enumerate(((gate_low, gr), (up_low, ur))):
            product = jnp.dot(narrow, right[l], preferred_element_type=F32).astype(BF16)
            for j in range(nt):
                val_out[i, j % 2, j // 2] = product[j * slab:(j + 1) * slab]
            pairs[i].start()
        sums = []
        for i in range(2):
            pairs[i].wait_recv()
            for j in range(chips):
                val_mid[i, j] = (
                    val_out[i, core, j].astype(F32) + pair_in[i, j].astype(F32)
                ).astype(BF16)
            start(values[i][0])
            val_in[i, chip] = val_mid[i, chip]
        for i in range(2):
            wait_recv(values[i][1])
            sums.append(jnp.sum(val_in[i].astype(F32), axis=0))
        gate_sum, up_sum = sums
        hid[t] = (gate_sum / (1.0 + jnp.exp(-gate_sum)) * up_sum).astype(BF16)
        start(hid_all[0])
        weights[4].wait()
        wait_recv(hid_all[1])

        down_part = contract_last(hid[...].reshape(span, width), dl[l])
        dlow_own[...] = (down_part * mask[l, 2]).astype(BF16)
        begin_down, arrive_down, finish_down = down_all
        begin_down()
        weights[5].wait()
        arrive_down()

        branch = jnp.zeros((span, f_block), F32)
        for kk in range(fan):
            at = kk * rank
            branch += contract_last(
                jnp.sum(dlow[:, kk].astype(F32), axis=0).astype(BF16), dr[l, :, at:at + rank]
            )
        br_out[...] = branch.astype(BF16).reshape(ns, rows, f_block)
        start(out_sum[0])
        br_in[s] = br_out[s]
        wait_recv(out_sum[1])
        finish()
        for p in range(nt):
            added = jnp.sum(br_in[:, :, p * piece:(p + 1) * piece].astype(F32), axis=0)
            own[p] = (own[p].astype(F32) + added).astype(BF16)

        wait_send(low_sum[0])
        wait_send(sq_sum[0])
        for i in range(2):
            pairs[i].wait_send()
            wait_send(values[i][0])
        wait_send(hid_all[0])
        finish_down()
        wait_send(out_sum[0])
        return carry

    lax.fori_loop(0, layers, layer, 0)
    wait_send(gain_send)
    wait_send(mask_sends)
    for p in range(nt):
        out[:, p * piece:(p + 1) * piece] = own[p]


def body(
    nt, ns,
    prompt, norm_gain, kept_ranks, gate_left, up_left, gate_right, up_right, down_left, down_right,
):
    rows, f_block = prompt.shape
    layers, rank, _ = gate_left.shape
    width = gate_right.shape[2]
    fan = nt // ns
    span = rows * ns
    slab = span // nt
    piece, chips = f_block // nt, nt // 2
    slots = max(nt, ns, ns * fan)
    weights = (gate_left, up_left, gate_right, up_right, down_left, down_right)
    vmem, hbm = pl.BlockSpec(memory_space=pltpu.VMEM), pl.BlockSpec(memory_space=pl.ANY)
    return pl.pallas_call(
        functools.partial(kernel, nt, ns, float(norm_gain.shape[1])),
        out_shape=jax.ShapeDtypeStruct((rows, f_block), BF16),
        in_specs=[vmem, vmem, pl.BlockSpec(memory_space=pltpu.SMEM)] + [hbm] * 6,
        out_specs=vmem,
        scratch_shapes=[pltpu.VMEM(w.shape, BF16) for w in weights] + [
            pltpu.VMEM((ns, fan, 1, f_block), F32),
            pltpu.VMEM((ns, fan, 1, f_block), F32),
            pltpu.VMEM((3, 1, rank), F32),
            pltpu.VMEM((ns, 3, 1, rank), F32),
            pltpu.VMEM((nt, rows, piece), BF16),
            pltpu.VMEM((nt, ns, fan, rows, piece), BF16),
            pltpu.VMEM((2, span, rank), BF16),
            pltpu.VMEM((ns, 2, span, rank), BF16),
            pltpu.VMEM((1, span), F32),
            pltpu.VMEM((ns, 1, span), F32),
            pltpu.VMEM((2, 2, chips, slab, width), BF16),
            pltpu.VMEM((2, chips, slab, width), BF16),
            pltpu.VMEM((2, chips, slab, width), BF16),
            pltpu.VMEM((2, chips, slab, width), BF16),
            pltpu.VMEM((nt, slab, width), BF16),
            pltpu.VMEM((span, rank), BF16),
            pltpu.VMEM((ns, fan, span, rank), BF16),
            pltpu.VMEM((ns, rows, f_block), BF16),
            pltpu.VMEM((ns, rows, f_block), BF16),
            pltpu.SemaphoreType.DMA((PHASES, slots)),
            pltpu.SemaphoreType.DMA((PHASES, slots)),
            pltpu.SemaphoreType.DMA((1, slots)),
            pltpu.SemaphoreType.DMA((1, slots)),
            pltpu.SemaphoreType.DMA((6, layers)),
        ],
        compiler_params=pltpu.CompilerParams(
            collective_id=0, has_side_effects=True, vmem_limit_bytes=52 * 1024 * 1024
        ),
        cost_estimate=pl.CostEstimate(
            flops=2 * span * sum(w.size for w in weights),
            bytes_accessed=2 * sum(w.size for w in weights),
            transcendentals=span * width * layers // nt,
        ),
    )(prompt, norm_gain, kept_ranks, *weights)


def solution(mesh):
    in_specs = (
        P(("groups", "section"), "tensor"),
        P(("groups", "section"), None),
        P(("groups", "section"), None),
    ) + (P("groups", "tensor", "section"),) * 6
    return jax.shard_map(
        functools.partial(body, mesh.shape["tensor"], mesh.shape["section"]),
        mesh=mesh, in_specs=in_specs, out_specs=P(("groups", "section"), "tensor"), check_vma=False,
    )
```

```python
import functools

import jax
import jax.numpy as jnp
from jax import lax
from jax.experimental import pallas as pl
from jax.experimental.pallas import tpu as pltpu
from jax.sharding import PartitionSpec as P

BF16, F32 = jnp.bfloat16, jnp.float32
AUX, SPREAD, GATHER, GATE_SUM, SQUARES, PAIR, GATE_VALUES, UP_VALUES = range(8)
HID_ALL, RELAY, DOWN, OUT_SUM, PHASES = range(8, 13)


def contract_last(left_side, right_side):
    return lax.dot_general(
        left_side, right_side, (((1,), (1,)), ((), ())), preferred_element_type=F32
    )


def kernel(
    nt, ns, features,
    prompt, norm_gain, kept, gl_hbm, ul_hbm, gr_hbm, ur_hbm, dl_hbm, dr_hbm,
    out,
    gl, ul, gr, ur, dl, dr,
    gain_out, gain, mask_out, mask,
    own, wide, low_out, low_in, sq_out, sq_in, val_out, pair_in, val_mid, val_in, hid,
    dlow_own, dlow, br_out, br_in,
    send, recv, mask_send, mask_recv, load,
):
    t, s = lax.axis_index("tensor"), lax.axis_index("section")
    layers = gl.shape[0]
    fan = nt // ns
    _, rows, piece = own.shape
    f_block = piece * nt
    span = rows * ns
    slab = hid.shape[1]
    rank = gl.shape[1]
    home, part = lax.div(t, fan), lax.rem(t, fan)
    chips = nt // 2
    chip, core = lax.div(t, 2), lax.rem(t, 2)
    sibling = chip * 2 + 1 - core

    def loads(l):
        return [
            pltpu.make_async_copy(h.at[l], v.at[l], load.at[i, l])
            for i, (h, v) in enumerate(
                ((gl_hbm, gl), (ul_hbm, ul), (gr_hbm, gr), (ur_hbm, ur), (dl_hbm, dl), (dr_hbm, dr))
            )
        ]

    def start_loads(l, carry):
        for copy in loads(l):
            copy.start()
        return carry

    lax.fori_loop(0, layers, start_loads, 0)

    count = nt * ns
    me = t * ns + s
    barrier = pltpu.get_barrier_semaphore()

    def greet(j, carry):
        peer = lax.rem(me + j, count)
        pl.semaphore_signal(
            barrier, inc=1,
            device_id={"tensor": lax.div(peer, ns), "section": lax.rem(peer, ns)},
            device_id_type=pl.DeviceIdType.MESH,
        )
        return carry

    lax.fori_loop(1, count, greet, 0)

    for j in range(ns):
        for kk in range(fan):
            at = (j * fan + kk) * f_block
            gain_out[j, kk] = norm_gain[:, at:at + f_block]
    position = t * rank + lax.broadcasted_iota(jnp.int32, (1, rank), 1)
    for i in range(3):
        mask_out[i] = jnp.where(position < kept[0, i], 1.0, 0.0).astype(F32)
    for p in range(nt):
        own[p] = prompt[:, p * piece:(p + 1) * piece]
    pl.semaphore_wait(barrier, count - 1)

    def copy_to(phase, src, dst, dest_slot, src_slot, tt, ss, sems=None):
        sender, receiver = (send, recv) if sems is None else sems
        return pltpu.make_async_remote_copy(
            src_ref=src, dst_ref=dst,
            send_sem=sender.at[phase, dest_slot], recv_sem=receiver.at[phase, src_slot],
            device_id={"tensor": tt, "section": ss}, device_id_type=pl.DeviceIdType.MESH,
        )

    def over_section(phase, src_of, dst_of, sems=None):
        sends, recvs = [], []
        for j in range(1, ns):
            peer = lax.rem(s + j, ns)
            sends.append(copy_to(phase, src_of(peer), dst_of(s), peer, s, t, peer, sems))
            recvs.append(copy_to(phase, src_of(peer), dst_of(peer), peer, peer, t, peer, sems))
        return sends, recvs

    def over_tensor(phase, src_of, dst_of):
        sends, recvs = [], []
        for j in range(1, nt):
            peer = lax.rem(t + j, nt)
            sends.append(copy_to(phase, src_of(peer), dst_of(t), peer, t, peer, s))
            recvs.append(copy_to(phase, src_of(peer), dst_of(peer), peer, peer, peer, s))
        return sends, recvs

    def pair_copies(i):
        return copy_to(PAIR, val_out.at[i, 1 - core], pair_in.at[i], i, i, sibling, s)

    def over_chips(phase, i):
        sends, recvs = [], []
        for j in range(1, chips):
            peer = lax.rem(chip + j, chips)
            src, to = val_mid.at[i, peer], peer * 2 + core
            sends.append(copy_to(phase, src, val_in.at[i, chip], peer, chip, to, s))
            recvs.append(copy_to(phase, src, val_in.at[i, peer], peer, peer, to, s))
        return sends, recvs

    def start(copies):
        for copy in copies:
            copy.start()

    def wait_recv(copies):
        for copy in copies:
            copy.wait_recv()

    def wait_send(copies):
        for copy in copies:
            copy.wait_send()

    def spread(phase, src_of, dst_of):
        is_home = home == s

        def each(action):
            for j in range(nt):
                peer = lax.rem(t + j, nt)
                copy = copy_to(
                    phase, src_of(peer), dst_of(peer).at[s, part], peer, s * fan + part, peer, home
                )
                if j == 0:
                    @pl.when(jnp.logical_not(is_home))
                    def _():
                        action(copy)
                else:
                    action(copy)

        def begin():
            each(lambda copy: copy.start())

            @pl.when(is_home)
            def _():
                dst_of(t)[s, part] = src_of(t)[...]

        def arrive():
            for j in range(ns):
                for kk in range(fan):
                    copy = copy_to(
                        phase, src_of(t), dst_of(t).at[j, kk], 0, j * fan + kk, s * fan + kk, j
                    )

                    @pl.when(jnp.logical_not((s * fan + kk == t) & (s == j)))
                    def _():
                        copy.wait_recv()

        def finish():
            each(lambda copy: copy.wait_send())

        return begin, arrive, finish

    gain_send, gain_recv = over_section(AUX, lambda j: gain_out.at[j], lambda j: gain.at[j])
    mask_sends, mask_recvs = over_section(
        0, lambda j: mask_out, lambda j: mask.at[j], (mask_send, mask_recv)
    )
    aux_first = spread(SPREAD, lambda j: own.at[j], lambda j: wide.at[j])
    gather = over_tensor(GATHER, lambda j: wide.at[t], lambda j: wide.at[j])
    low_sum = over_section(GATE_SUM, lambda j: low_out, lambda j: low_in.at[j])
    sq_sum = over_section(SQUARES, lambda j: sq_out, lambda j: sq_in.at[j])
    pairs = [pair_copies(i) for i in range(2)]
    values = [over_chips(GATE_VALUES, 0), over_chips(UP_VALUES, 1)]
    mine, theirs = hid.at[t], hid.at[sibling]
    others = [lax.rem(chip + j, chips) for j in range(1, chips)]
    hid_far = [copy_to(HID_ALL, mine, mine, p * 2 + core, t, p * 2 + core, s) for p in others]
    hid_near = copy_to(HID_ALL, mine, mine, sibling, t, sibling, s)
    far_in, relays, relays_in = [], [], []
    for p in others:
        got, due = p * 2 + core, p * 2 + 1 - core
        far_in.append(copy_to(HID_ALL, mine, hid.at[got], got, got, got, s))
        relays.append(copy_to(RELAY, hid.at[got], hid.at[got], p, p, sibling, s))
        relays_in.append(copy_to(RELAY, hid.at[due], hid.at[due], p, p, sibling, s))
    near_in = copy_to(HID_ALL, mine, theirs, sibling, sibling, sibling, s)
    down_all = spread(DOWN, lambda j: dlow_own, lambda j: dlow)
    out_sum = over_section(OUT_SUM, lambda j: br_out.at[j], lambda j: br_in.at[j])

    start(gain_send)
    start(mask_sends)
    gain[s] = gain_out[s]
    mask[s] = mask_out[...]

    def layer(l, carry):
        begin, arrive, finish = aux_first
        begin()

        @pl.when(l == 0)
        def _():
            wait_recv(gain_recv)
            wait_recv(mask_recvs)

        weights = loads(l)
        weights[0].wait()
        weights[1].wait()
        arrive()

        start(gather[0])
        gate_part = jnp.zeros((span, rank), F32)
        up_part = jnp.zeros((span, rank), F32)
        squares = jnp.zeros((span, 1), F32)
        wait_recv(gather[1])
        for p in range(nt):
            for kk in range(fan):
                values_here = wide[p, :, kk].reshape(span, piece).astype(F32)
                squares += jnp.sum(values_here * values_here, axis=-1, keepdims=True)
                at = kk * f_block + p * piece
                gains = gain[l, kk, :, p * piece:(p + 1) * piece]
                scaled = (values_here * gains).astype(BF16)
                gate_part += contract_last(scaled, gl[l, :, at:at + piece])
                up_part += contract_last(scaled, ul[l, :, at:at + piece])
        low_out[0] = gate_part.astype(BF16)
        low_out[1] = up_part.astype(BF16)
        diagonal = lax.broadcasted_iota(jnp.int32, (span, span), 0) == lax.broadcasted_iota(
            jnp.int32, (span, span), 1
        )
        sq_out[...] = jnp.sum(jnp.where(diagonal, squares, 0.0), axis=0, keepdims=True)
        start(sq_sum[0])
        start(low_sum[0])
        low_in[s] = low_out[...]
        sq_in[s] = sq_out[...]
        wait_recv(sq_sum[1])
        square_row = jnp.sum(sq_in[...], axis=0)
        square = jnp.sum(jnp.where(diagonal, square_row, 0.0), axis=1, keepdims=True)
        scale = lax.rsqrt(square / features + 1e-05)
        weights[2].wait()
        weights[3].wait()
        wait_recv(low_sum[1])
        total = jnp.sum(low_in[...].astype(F32), axis=0)
        gate_low = (total[0] * scale * mask[l, 0]).astype(BF16)
        up_low = (total[1] * scale * mask[l, 1]).astype(BF16)

        width = gr.shape[2]
        wait_send(gather[0])
        for i, (narrow, right) in enumerate(((gate_low, gr), (up_low, ur))):
            product = jnp.dot(narrow, right[l], preferred_element_type=F32).astype(BF16)
            for j in range(nt):
                val_out[i, j % 2, j // 2] = product[j * slab:(j + 1) * slab]
            pairs[i].start()
        sums = []
        for i in range(2):
            pairs[i].wait_recv()
            for j in range(chips):
                val_mid[i, j] = (
                    val_out[i, core, j].astype(F32) + pair_in[i, j].astype(F32)
                ).astype(BF16)
            start(values[i][0])
            val_in[i, chip] = val_mid[i, chip]
        for i in range(2):
            wait_recv(values[i][1])
            sums.append(jnp.sum(val_in[i].astype(F32), axis=0))
        gate_sum, up_sum = sums
        hid[t] = (gate_sum / (1.0 + jnp.exp(-gate_sum)) * up_sum).astype(BF16)
        start(hid_far)
        hid_near.start()
        weights[4].wait()
        for arrived, relay in zip(far_in, relays):
            arrived.wait_recv()
            relay.start()
        near_in.wait_recv()
        wait_recv(relays_in)

        down_part = contract_last(hid[...].reshape(span, width), dl[l])
        dlow_own[...] = (down_part * mask[l, 2]).astype(BF16)
        begin_down, arrive_down, finish_down = down_all
        wait_send(relays)
        begin_down()
        weights[5].wait()
        arrive_down()

        branch = jnp.zeros((span, f_block), F32)
        for kk in range(fan):
            at = kk * rank
            branch += contract_last(
                jnp.sum(dlow[:, kk].astype(F32), axis=0).astype(BF16), dr[l, :, at:at + rank]
            )
        br_out[...] = branch.astype(BF16).reshape(ns, rows, f_block)
        start(out_sum[0])
        br_in[s] = br_out[s]
        wait_recv(out_sum[1])
        finish()
        for p in range(nt):
            added = jnp.sum(br_in[:, :, p * piece:(p + 1) * piece].astype(F32), axis=0)
            own[p] = (own[p].astype(F32) + added).astype(BF16)

        wait_send(low_sum[0])
        wait_send(sq_sum[0])
        for i in range(2):
            pairs[i].wait_send()
            wait_send(values[i][0])
        wait_send(hid_far)
        hid_near.wait_send()
        finish_down()
        wait_send(out_sum[0])
        return carry

    lax.fori_loop(0, layers, layer, 0)
    wait_send(gain_send)
    wait_send(mask_sends)
    for p in range(nt):
        out[:, p * piece:(p + 1) * piece] = own[p]


def body(
    nt, ns,
    prompt, norm_gain, kept_ranks, gate_left, up_left, gate_right, up_right, down_left, down_right,
):
    rows, f_block = prompt.shape
    layers, rank, _ = gate_left.shape
    width = gate_right.shape[2]
    fan = nt // ns
    span = rows * ns
    slab = span // nt
    piece, chips = f_block // nt, nt // 2
    slots = max(nt, ns, ns * fan)
    weights = (gate_left, up_left, gate_right, up_right, down_left, down_right)
    vmem, hbm = pl.BlockSpec(memory_space=pltpu.VMEM), pl.BlockSpec(memory_space=pl.ANY)
    return pl.pallas_call(
        functools.partial(kernel, nt, ns, float(norm_gain.shape[1])),
        out_shape=jax.ShapeDtypeStruct((rows, f_block), BF16),
        in_specs=[vmem, vmem, pl.BlockSpec(memory_space=pltpu.SMEM)] + [hbm] * 6,
        out_specs=vmem,
        scratch_shapes=[pltpu.VMEM(w.shape, BF16) for w in weights] + [
            pltpu.VMEM((ns, fan, 1, f_block), F32),
            pltpu.VMEM((ns, fan, 1, f_block), F32),
            pltpu.VMEM((3, 1, rank), F32),
            pltpu.VMEM((ns, 3, 1, rank), F32),
            pltpu.VMEM((nt, rows, piece), BF16),
            pltpu.VMEM((nt, ns, fan, rows, piece), BF16),
            pltpu.VMEM((2, span, rank), BF16),
            pltpu.VMEM((ns, 2, span, rank), BF16),
            pltpu.VMEM((1, span), F32),
            pltpu.VMEM((ns, 1, span), F32),
            pltpu.VMEM((2, 2, chips, slab, width), BF16),
            pltpu.VMEM((2, chips, slab, width), BF16),
            pltpu.VMEM((2, chips, slab, width), BF16),
            pltpu.VMEM((2, chips, slab, width), BF16),
            pltpu.VMEM((nt, slab, width), BF16),
            pltpu.VMEM((span, rank), BF16),
            pltpu.VMEM((ns, fan, span, rank), BF16),
            pltpu.VMEM((ns, rows, f_block), BF16),
            pltpu.VMEM((ns, rows, f_block), BF16),
            pltpu.SemaphoreType.DMA((PHASES, slots)),
            pltpu.SemaphoreType.DMA((PHASES, slots)),
            pltpu.SemaphoreType.DMA((1, slots)),
            pltpu.SemaphoreType.DMA((1, slots)),
            pltpu.SemaphoreType.DMA((6, layers)),
        ],
        compiler_params=pltpu.CompilerParams(
            collective_id=0, has_side_effects=True, vmem_limit_bytes=52 * 1024 * 1024
        ),
        cost_estimate=pl.CostEstimate(
            flops=2 * span * sum(w.size for w in weights),
            bytes_accessed=2 * sum(w.size for w in weights),
            transcendentals=span * width * layers // nt,
        ),
    )(prompt, norm_gain, kept_ranks, *weights)


def solution(mesh):
    in_specs = (
        P(("groups", "section"), "tensor"),
        P(("groups", "section"), None),
        P(("groups", "section"), None),
    ) + (P("groups", "tensor", "section"),) * 6
    return jax.shard_map(
        functools.partial(body, mesh.shape["tensor"], mesh.shape["section"]),
        mesh=mesh, in_specs=in_specs, out_specs=P(("groups", "section"), "tensor"), check_vma=False,
    )
```
